256 devices in a mesh: expert: 32 (over x, z), row: 8 (over y, core).
Axes of the slice: x: 4, y: 4, z: 8, core: 2. Of those that a mesh axis runs over, the one named last changes fastest.
Arguments:
- tokens: bfloat16 [8192, 7168], P('expert', 'row'), may hold values from -6 to 6
- routing: int32 [8192, 8], P('expert'), may hold values from 0 to 255, all different within a row; in each aligned block of 256 rows (0 to 255, 256 to 511, ...) at most 12 rows name the same one
- weights: bfloat16 [256, 2048, 256], P('expert', 'row'), may hold values from -6 to 6
- indices: int32 [256, 2048, 128], P('expert', 'row'), may hold values from 0 to 63
- codebook: bfloat16 [256, 2, 64], P('expert'), may hold values from -5 to 5
- hinv_panel: float32 [256, 256, 256], P(('expert', 'row')), may hold values from -1.6 to 2, as said below
Outputs:
- hessian: float32 [256, 7168, 256], P('expert', 'row')
- errors: float32 [256, 2048, 256], P('expert', 'row')
The draws below stay inside these ranges and needn't reach their ends.
Inputs may be any that keep to these rules, and one draw needn't show every extreme that they name: `routing`: each token names 8 different experts; within each aligned block of 256 tokens (the tokens of one index of the expert axis) no expert is named by more than 12 tokens, a bound that some block reaches; every expert is named by some token. `hinv_panel`: upper triangular with positive diagonal entries.
All inputs are finite; a program needn't handle non-finite values.
Results may differ from the reference program's by a relative error of at most 0.0003.
Values may be sent and summed in bfloat16 or wider, within the bound.
No kernel may reach another device: no remote copies, remote signals or barrier semaphores. Data moves between devices by JAX's collectives and lax.ppermute only.
A program may use at most 192 MiB of HBM per device.

```python
import math
import jax
import jax.numpy as jnp
import numpy as np
from jax import lax

D = 7168
FF = 2048
TOP = 8
TOK_DEV = 256
K = 64
EXPERTS = 256
TOKENS = 8192
CAP = 12
PW = 256
N_EXPERT = 32


def draw_hinv_panel(key, part):
    key = jax.random.fold_in(key, 17)
    key_diag, key_upper = jax.random.split(key)
    diagonal = jnp.exp(jax.random.uniform(key_diag, (EXPERTS, PW), jnp.float32, math.log(0.5), math.log(2.0)))
    spread_off = jax.random.uniform(key_upper, (EXPERTS, PW, PW), jnp.float32, -1.0, 1.0)
    position = jnp.arange(PW)
    above = (position[:, None] < position[None, :]).astype(jnp.float32)
    column_scale = 0.8 / jnp.maximum(position, 1).astype(jnp.float32)
    upper_part = spread_off * above[None, :, :] * (diagonal[:, None, :] * column_scale[None, None, :])
    return upper_part + diagonal[:, :, None] * jnp.eye(PW, dtype=jnp.float32)[None, :, :]


def with_ends(entries, stream_key, smallest, high):
    place = [jax.random.randint(jax.random.fold_in(stream_key, axis), (), 0, length) for axis, length in enumerate(entries.shape)]
    main_axis = entries.shape.index(max(entries.shape))
    next_to = place[:main_axis] + [(place[main_axis] + 1) % entries.shape[main_axis]] + place[main_axis + 1:]
    return entries.at[tuple(place)].set(smallest).at[tuple(next_to)].set(high)


def block_scale(rng, shape, cuts, least, top_value):
    factor_of = 1.0
    for dim, shards_of in cuts:
        draws = jax.random.uniform(jax.random.fold_in(jax.random.fold_in(rng, 6), dim), (shards_of,), jnp.float32, least / len(cuts), top_value / len(cuts))
        factor_of = factor_of * jnp.repeat(jnp.exp(draws), shape[dim] // shards_of).reshape((-1,) + (1,) * (len(shape) - 1 - dim))
    return factor_of


def routed_block(key, own, number, rows, number_of, top, limit, skew):
    ranking = jax.random.permutation(key, number_of)
    packed, ordinary = portions_of(number_of, rows * top, limit, skew, True), portions_of(number_of, rows * top, limit, skew, False)
    places = jnp.arange(number_of)

    def named(tallies, turn):
        used = int((tallies > 0).sum())
        fixed = max(1, used // 4)
        passed = fixed + (places - fixed + turn * (used - fixed)) % max(1, number_of - fixed)
        return jnp.zeros((number_of,), jnp.int32).at[ranking[jnp.where(places < fixed, places, passed)]].set(jnp.asarray(tallies, jnp.int32))

    tallies = jnp.where(number % 4 == 0, named(packed, number // 4), named(ordinary, number - number // 4 - 1))
    mixed = jax.random.permutation(jax.random.fold_in(own, 3), number_of)
    giver, receiver = mixed[0:number_of // 2 * 2:2], mixed[1:number_of // 2 * 2:2]
    slack = jnp.minimum(tallies[giver] - 1, limit - tallies[receiver]) // 2
    slack = jnp.where((giver == ranking[0]) | (receiver == ranking[0]) | (tallies[receiver] == 0), 0, jnp.maximum(slack, 0))
    passed = jax.random.randint(jax.random.fold_in(own, 4), (number_of // 2,), 0, 1 << 20) % (slack + 1)
    tallies = tallies.at[giver].add(-passed).at[receiver].add(passed)
    items = jnp.searchsorted(jnp.cumsum(tallies), jnp.arange(rows * top), side="right").astype(jnp.int32)
    table = items.reshape(top, rows).T
    table = table[jax.random.permutation(jax.random.fold_in(own, 1), rows)]
    turn = jax.random.randint(jax.random.fold_in(own, 2), (rows, 1), 0, top)
    return jnp.take_along_axis(table, (jnp.arange(top)[None, :] + turn) % top, axis=1)


def portions_of(number_of, total, limit, slope, full):
    weights = [(1 << 20) // math.isqrt(grade ** slope) + 1 for grade in range(1, number_of + 1)]
    largest = limit if full else min(limit, max(-(-total // number_of), total * weights[0] // sum(weights)))
    least = 1 if total - largest >= number_of - 1 else 0
    given, rest = [largest] + [least] * (number_of - 1), total - largest - least * (number_of - 1)
    while rest > 0:
        movable = [i for i in range(1, number_of) if given[i] < largest] or [i for i in range(1, number_of) if given[i] < limit]
        pool, left = sum([weights[i] for i in movable]), rest
        for i in movable:
            extra = min(limit - given[i], max(1, left * weights[i] // pool), rest)
            given[i] = given[i] + extra
            rest = rest - extra
    return np.array(given)


def normal_values(key, dims, deviation, bound, cuts=(), kind=jnp.bfloat16):
    result = jax.random.normal(key, dims, jnp.float32) * deviation
    if len(cuts) > 0:
        result = block_scale(key, dims, cuts, -0.22, 0.18) * result
    return jnp.clip(result, min=-bound, max=bound).astype(kind)


def setup_inputs(seed: int = 0) -> dict:
    key_of = jax.random.split(jax.random.key(seed), 7)
    tokens = normal_values(key_of[0], (TOKENS, D), 1.0, 6.0, ((0, 32), (1, 8)))
    routing_keys = jax.random.split(jax.random.fold_in(key_of[1], 1), TOKENS // TOK_DEV)
    routing_turns = jax.random.permutation(jax.random.fold_in(key_of[1], 3), TOKENS // TOK_DEV)
    routing = jax.vmap(lambda own, number: routed_block(jax.random.fold_in(key_of[1], 2), own, number, TOK_DEV, EXPERTS, TOP, CAP, 2))(routing_keys, routing_turns).reshape((TOKENS, TOP))
    weights = normal_values(key_of[2], (EXPERTS, FF, PW), 1.0, 6.0, ((0, 32), (1, 8)))
    indices = with_ends(jax.random.randint(key_of[3], (EXPERTS, FF, PW // 2), 0, K), jax.random.fold_in(key_of[3], 1), 0, K - 1).astype(jnp.int32)
    codebook = normal_values(key_of[4], (EXPERTS, 2, K), 1.0, 5.0, ((0, 32),))
    hinv_panel = draw_hinv_panel(jax.random.fold_in(key_of[6], 71), 0)
    return dict(tokens=tokens, routing=routing, weights=weights, indices=indices, codebook=codebook, hinv_panel=hinv_panel)


def reference(tokens, routing, weights, indices, codebook, hinv_panel):
    labels = jnp.arange(EXPERTS, dtype=jnp.int32)
    member = jnp.any(routing[:, :, None] == labels[None, None, :], axis=1)
    counts = jnp.sum(member.astype(jnp.float32), axis=0)
    most_rows = N_EXPERT * CAP

    def one_expert(expert_id):
        column = member[:, expert_id]
        picked, = jnp.nonzero(column, size=most_rows, fill_value=0)
        usable = jnp.arange(most_rows, dtype=jnp.int32) < jnp.sum(column.astype(jnp.int32))
        chosen = jnp.where(usable[:, None], tokens[picked.astype(jnp.int32)], jnp.zeros((), tokens.dtype))
        product = jnp.dot(chosen.T.astype(jnp.float32), chosen[:, :PW].astype(jnp.float32), preferred_element_type=jnp.float32)
        return product * (2.0 / counts[expert_id])
    hessian = lax.map(one_expert, labels)

    def lookup(book_rows, picked_ids):
        return book_rows[:, picked_ids]
    coords = jax.vmap(lookup)(codebook, indices)
    decoded = jnp.moveaxis(coords, 1, -1).reshape(EXPERTS, FF, PW)
    residual = weights.astype(jnp.float32) - decoded.astype(jnp.float32)
    errors = lax.linalg.triangular_solve(hinv_panel, residual, left_side=False, lower=False)
    return (hessian, errors)
```

```python
import functools

import jax
import jax.numpy as jnp
from jax import lax
from jax.experimental import pallas as pl
from jax.experimental.pallas import tpu as pltpu
from jax.sharding import Mesh, PartitionSpec as P

NX, NZ, NY, NC = 4, 8, 4, 2
EXP_DEV = 8
CAP = 12
TOK = 256
LANES = 128
FEAT = 896
ROWS = TOK + 16
WROWS = TOK + 32
CHUNKS = ((0,), (-1, 1), (-2, 2), (-3, 3), (4,))
SLOTS = NZ * EXP_DEV * CAP
WMSG = SLOTS + 16
F32 = jnp.float32
BF16 = jnp.bfloat16
VMEM_LIMIT = 48 * 1024 * 1024


def params():
    return pltpu.CompilerParams(vmem_limit_bytes=VMEM_LIMIT)


def vmem():
    return pl.BlockSpec(memory_space=pltpu.VMEM)


def smem():
    return pl.BlockSpec(memory_space=pltpu.SMEM)


def cost(flops, moved):
    return pl.CostEstimate(flops=flops, bytes_accessed=moved, transcendentals=0)


def routing_rows(routing_t):
    listed = routing_t.astype(F32)
    return jnp.concatenate([listed, jnp.full(listed.shape, -1.0, F32)], axis=0).astype(BF16)


def payload_kernel(tokens_ref, routing_ref, out_ref):
    out_ref[0:TOK, :] = tokens_ref[...]
    out_ref[TOK:ROWS, :] = jnp.zeros((16, FEAT), BF16)
    out_ref[TOK:ROWS, 0:TOK] = routing_rows(routing_ref[...])


def window_payload_kernel(place_ref, tokens_ref, routing_ref, got_ref, out_ref):
    first = place_ref[2] == 0

    @pl.when(first)
    def _():
        out_ref[0:TOK, :] = tokens_ref[:, 0:LANES]

    @pl.when(jnp.logical_not(first))
    def _():
        out_ref[0:TOK, :] = got_ref[...]

    listed = routing_rows(routing_ref[...])
    out_ref[TOK:TOK + 16, :] = listed[:, 0:LANES]
    out_ref[TOK + 16:WROWS, :] = listed[:, LANES:TOK]


def ranks(listed, x_index, z_index):
    line = lax.broadcasted_iota(jnp.int32, (NX * EXP_DEV, TOK), 0)
    label = EXP_DEV * (((x_index + line // EXP_DEV) % NX) * NZ + z_index) + line % EXP_DEV
    label = label.astype(F32)
    member = jnp.zeros((NX * EXP_DEV, TOK), F32)
    for slot in range(8):
        member = member + jnp.where(listed[slot:slot + 1, :] == label, 1.0, 0.0)
    row = lax.broadcasted_iota(jnp.int32, (TOK, TOK), 0)
    column = lax.broadcasted_iota(jnp.int32, (TOK, TOK), 1)
    upto = jnp.where(row <= column, 1.0, 0.0).astype(BF16)
    running = jnp.dot(member.astype(BF16), upto, preferred_element_type=F32)
    return member, member * running


def selectors(rank, count, spot):
    size = count * EXP_DEV * CAP
    shape = (NX * size, NX * EXP_DEV)
    row = lax.broadcasted_iota(jnp.int32, shape, 0)
    column = lax.broadcasted_iota(jnp.int32, shape, 1)
    inside = row % size
    if count == 1:
        expert = inside // CAP
        mine = row >= 0
    else:
        expert = 2 * (inside // (2 * count * CAP)) + (inside % (2 * CAP)) // CAP
        mine = (inside // (2 * CAP)) % count == spot
    match = jnp.logical_and(column == (row // size) * EXP_DEV + expert, mine)
    spread = jnp.where(match, 1.0, 0.0).astype(BF16)
    wide = jnp.dot(spread, rank.astype(BF16), preferred_element_type=F32)
    want = (lax.broadcasted_iota(jnp.int32, (NX * size, TOK), 0) % CAP + 1).astype(F32)
    return jnp.where(wide == want, 1.0, 0.0).astype(BF16)


def pack_kernel(count, place_ref, *refs):
    blocks, outs = refs[:count], refs[count:]
    size = count * EXP_DEV * CAP
    total = None
    for spot, block in enumerate(blocks):
        listed = block[TOK:ROWS, 0:TOK].astype(F32)
        _, rank = ranks(listed, place_ref[0], place_ref[1])
        picked = jnp.dot(
            selectors(rank, count, spot), block[0:TOK, :], preferred_element_type=F32
        )
        total = picked if total is None else total + picked
    for k, out in enumerate(outs):
        out[...] = total[k * size:(k + 1) * size, :].astype(BF16)


def pack(place, blocks):
    count = len(blocks)
    size = count * EXP_DEV * CAP
    return pl.pallas_call(
        functools.partial(pack_kernel, count),
        out_shape=[jax.ShapeDtypeStruct((size, FEAT), BF16)] * NX,
        in_specs=[smem()] + [vmem()] * count,
        out_specs=[vmem()] * NX,
        compiler_params=params(),
        cost_estimate=cost(2 * NX * size * TOK * FEAT * count, 2 * FEAT * (ROWS * count + NX * size)),
        name="pack_%d" % count,
    )(place, *blocks)


def window_kernel(place_ref, gathered_ref, *outs):
    x_index, z_index = place_ref[0], place_ref[1]
    start = 0
    counts = jnp.zeros((NX * EXP_DEV, LANES), F32)
    for chunk in CHUNKS:
        count = len(chunk)
        size = count * EXP_DEV * CAP
        total = None
        for spot, offset in enumerate(chunk):
            block = gathered_ref[(z_index + offset + NZ) % NZ]
            listed = jnp.concatenate(
                [block[TOK:TOK + 16, :], block[TOK + 16:WROWS, :]], axis=1
            ).astype(F32)
            member, rank = ranks(listed, x_index, z_index)
            counts = counts + jnp.sum(member, axis=1, keepdims=True)
            picked = jnp.dot(
                selectors(rank, count, spot), block[0:TOK, :], preferred_element_type=F32
            )
            total = picked if total is None else total + picked
        for k, out in enumerate(outs):
            out[start:start + size, :] = total[k * size:(k + 1) * size, :].astype(BF16)
        start += size
    for k, out in enumerate(outs):
        mine = counts[k * EXP_DEV:(k + 1) * EXP_DEV, :]
        out[SLOTS:WMSG, :] = jnp.concatenate([mine, mine], axis=0).astype(BF16)


def inverse_kernel(factor_ref, out_ref):
    width = factor_ref.shape[-1]
    factor = factor_ref[0]
    row = lax.broadcasted_iota(jnp.int32, (width, width), 0)
    column = lax.broadcasted_iota(jnp.int32, (width, width), 1)
    diagonal = jnp.where(row == column, factor, 0.0)
    across = 1.0 / jnp.sum(diagonal, axis=0, keepdims=True)
    down = 1.0 / jnp.sum(diagonal, axis=1, keepdims=True)

    def level(span):
        return jnp.where(
            jnp.logical_and(
                row // (2 * span) == column // (2 * span),
                jnp.logical_and(row // span % 2 == 0, column // span % 2 == 1),
            ),
            factor,
            0.0,
        )

    result = jnp.where(row == column, across, 0.0) - down * level(1) * across
    span = 2
    while span < width:
        first = jnp.dot(result, level(span), precision=lax.Precision.HIGHEST, preferred_element_type=F32)
        result = result - jnp.dot(first, result, precision=lax.Precision.HIGHEST, preferred_element_type=F32)
        span *= 2
    out_ref[0] = result


def split(value):
    high = value.astype(BF16)
    return high, (value - high.astype(F32)).astype(BF16)


def errors_kernel(weights_ref, indices_ref, codebook_ref, inverse_ref, out_ref):
    picked = indices_ref[0]
    rows, pairs = picked.shape
    book = codebook_ref[0].astype(F32)
    book = jnp.concatenate([book, jnp.zeros(book.shape, F32)], axis=1)
    coords = [
        jnp.take_along_axis(jnp.broadcast_to(book[c:c + 1, :], (rows, pairs)), picked, axis=1)
        for c in range(2)
    ]
    both = jnp.concatenate(coords, axis=1).astype(BF16)
    row = lax.broadcasted_iota(jnp.int32, (2 * pairs, 2 * pairs), 0)
    column = lax.broadcasted_iota(jnp.int32, (2 * pairs, 2 * pairs), 1)
    weave = jnp.where(column == 2 * (row % pairs) + row // pairs, 1.0, 0.0).astype(BF16)
    decoded = jnp.dot(both, weave, preferred_element_type=F32)
    residual_high, residual_low = split(weights_ref[0].astype(F32) - decoded)
    inverse_high, inverse_low = split(inverse_ref[0])
    total = jnp.dot(residual_low, inverse_high, preferred_element_type=F32)
    total = total + jnp.dot(residual_high, inverse_low, preferred_element_type=F32)
    out_ref[0] = total + jnp.dot(residual_high, inverse_high, preferred_element_type=F32)


def hessian_kernel(place_ref, *refs):
    messages, (mine_ref, other_ref, out_ref) = refs[:-3], refs[-3:]
    pair = pl.program_id(0)
    first = place_ref[2] == 0
    features, windows = [], []
    row = lax.broadcasted_iota(jnp.int32, (4 * CAP, TOK), 0)
    single = (row // CAP - 2 * (pair % 2), row // CAP - 2 * (pair % 2))
    double = (row % (2 * CAP)) // CAP
    for k in range(NX):
        start = k * WMSG
        for c, chunk in enumerate(CHUNKS):
            features.append(messages[k * len(CHUNKS) + c][...])
            if len(chunk) == 1:
                begin, owner = start + 4 * CAP * (pair // 2), single[0]
            else:
                begin, owner = start + 4 * CAP * pair, double
            where = pl.ds(pl.multiple_of(begin, 16), 4 * CAP)
            near, far = mine_ref[where, :].astype(F32), other_ref[where, :].astype(F32)
            both = jnp.concatenate(
                [jnp.where(first, near, far), jnp.where(first, far, near)], axis=1
            )
            windows.append(
                jnp.concatenate(
                    [jnp.where(owner == e, both, 0.0) for e in range(2)], axis=1
                ).astype(BF16)
            )
            start += len(chunk) * EXP_DEV * CAP
    product = lax.dot_general(
        jnp.concatenate(features, axis=0),
        jnp.concatenate(windows, axis=0),
        (((0,), (0,)), ((), ())),
        preferred_element_type=F32,
    )
    counts = jnp.zeros((16, LANES), F32)
    for k in range(NX):
        counts = counts + mine_ref[k * WMSG + SLOTS:(k + 1) * WMSG, :].astype(F32)
    line = lax.broadcasted_iota(jnp.int32, (16, LANES), 0)
    for e in range(2):
        count = jnp.sum(jnp.where(line == 2 * pair + e, counts, 0.0), axis=0, keepdims=True)
        scale = 2.0 / count
        scale = jnp.concatenate([scale, scale], axis=1)
        out_ref[e] = product[:, e * TOK:(e + 1) * TOK] * scale


def shifted(size, step):
    return [(i, (i + step) % size) for i in range(size)]


def x_pairs(step):
    return [
        ((a * NY) * NC + c, (((a + step) % NX) * NY) * NC + c) for a in range(NX) for c in range(NC)
    ]


def local(tokens, routing, weights, indices, codebook, hinv_panel):
    x_index, z_index = lax.axis_index("x"), lax.axis_index("z")
    y_index, core = lax.axis_index("y"), lax.axis_index("core")
    place = jnp.stack([x_index, z_index, core]).astype(jnp.int32)
    routing_t = routing.T
    half = lax.ppermute(tokens[:, LANES:2 * LANES], "core", [(0, 1)])
    payload = pl.pallas_call(
        payload_kernel,
        out_shape=jax.ShapeDtypeStruct((ROWS, FEAT), BF16),
        in_specs=[vmem()] * 2,
        out_specs=vmem(),
        compiler_params=params(),
        cost_estimate=cost(0, 4 * ROWS * FEAT),
        name="payload",
    )(tokens, routing_t)
    window_payload = pl.pallas_call(
        window_payload_kernel,
        out_shape=jax.ShapeDtypeStruct((WROWS, LANES), BF16),
        in_specs=[smem()] + [vmem()] * 3,
        out_specs=vmem(),
        compiler_params=params(),
        name="window_payload",
    )(place, tokens, routing_t, half)
    gathered = lax.all_gather(window_payload, "z", axis=0, tiled=False)
    forward, backward = [payload], [payload]
    for step in range(1, 5):
        forward.append(lax.ppermute(forward[-1], "z", shifted(NZ, 1)))
        if step < 4:
            backward.append(lax.ppermute(backward[-1], "z", shifted(NZ, -1)))
    chunks = [[payload]] + [[forward[s], backward[s]] for s in (1, 2, 3)] + [[forward[4]]]
    messages = [[None] * len(CHUNKS) for _ in range(NX)]
    for c, blocks in enumerate(chunks):
        packed = pack(place, blocks)
        messages[0][c] = packed[0]
        for k in (2, 1, 3):
            messages[k][c] = lax.ppermute(packed[k], "x", shifted(NX, k))

    inverse = pl.pallas_call(
        inverse_kernel,
        out_shape=jax.ShapeDtypeStruct(hinv_panel.shape, F32),
        in_specs=[vmem()],
        out_specs=vmem(),
        compiler_params=params(),
        cost_estimate=cost(14 * 6 * 2 * TOK ** 3, 8 * TOK * TOK),
        name="inverse",
    )(hinv_panel)
    inverses = lax.all_gather(inverse, ("y", "core"), axis=0, tiled=True)
    experts, rows, width = weights.shape
    pairs = indices.shape[2]
    errors = pl.pallas_call(
        errors_kernel,
        grid=(experts,),
        out_shape=jax.ShapeDtypeStruct(weights.shape, F32),
        in_specs=[
            pl.BlockSpec((1, rows, width), lambda e: (e, 0, 0)),
            pl.BlockSpec((1, rows, pairs), lambda e: (e, 0, 0)),
            pl.BlockSpec((1,) + codebook.shape[1:], lambda e: (e, 0, 0)),
            pl.BlockSpec((1, width, width), lambda e: (e, 0, 0)),
        ],
        out_specs=pl.BlockSpec((1, rows, width), lambda e: (e, 0, 0)),
        compiler_params=params(),
        cost_estimate=cost(8 * experts * rows * width * width, experts * rows * width * 12),
        name="errors",
    )(weights, indices, codebook, inverses)

    window_parts = pl.pallas_call(
        window_kernel,
        out_shape=[jax.ShapeDtypeStruct((WMSG, LANES), BF16)] * NX,
        in_specs=[smem(), vmem()],
        out_specs=[vmem()] * NX,
        compiler_params=params(),
        cost_estimate=cost(2 * NX * 2 * SLOTS * TOK * LANES, 4 * NX * WMSG * LANES),
        name="window_pack",
    )(place, gathered)
    arrived = [window_parts[0]] + [
        lax.ppermute(window_parts[k], ("x", "y", "core"), x_pairs(k)) for k in (1, 2, 3)
    ]
    low = jnp.concatenate(arrived[:2], axis=0)
    high = jnp.concatenate(arrived[2:], axis=0)
    up_low = lax.ppermute(low, "y", [(0, 1)])
    down_high = lax.ppermute(high, "y", [(0, 3)])
    up = lax.ppermute(jnp.where(y_index == 0, high, up_low), "y", [(0, 1), (1, 2)])
    down = lax.ppermute(jnp.where(y_index == 0, low, down_high), "y", [(0, 3), (3, 2)])
    low = jnp.where(y_index == 0, low, jnp.where(y_index == 1, up_low, jnp.where(y_index == 2, up, down)))
    high = jnp.where(y_index == 0, high, jnp.where(y_index == 1, up, jnp.where(y_index == 2, down, down_high)))
    mine = jnp.concatenate([low, high], axis=0)
    other = lax.ppermute(mine, "core", shifted(NC, 1))

    operands, specs = [], []
    for k in range(NX):
        for c, chunk in enumerate(CHUNKS):
            operands.append(messages[k][c])
            if len(chunk) == 1:
                specs.append(pl.BlockSpec((4 * CAP, FEAT), lambda p: (p // 2, 0)))
            else:
                specs.append(pl.BlockSpec((4 * CAP, FEAT), lambda p: (p, 0)))
    full = pl.BlockSpec((NX * WMSG, LANES), lambda p: (0, 0))
    hessian = pl.pallas_call(
        hessian_kernel,
        grid=(EXP_DEV // 2,),
        out_shape=jax.ShapeDtypeStruct((EXP_DEV, FEAT, TOK), F32),
        in_specs=[smem()] + specs + [full, full],
        out_specs=pl.BlockSpec((2, FEAT, TOK), lambda p: (p, 0, 0)),
        compiler_params=params(),
        cost_estimate=cost(8 * 960 * FEAT * 2 * TOK, 4 * EXP_DEV * FEAT * TOK + 2 * NX * SLOTS * FEAT),
        name="hessian",
    )(place, *operands, mine, other)
    return hessian, errors


def solution(mesh):
    grid = Mesh(mesh.devices.reshape(NX, NZ, NY, NC), ("x", "z", "y", "core"))
    expert, row = ("x", "z"), ("y", "core")
    in_specs = (
        P(expert, row),
        P(expert, None),
        P(expert, row, None),
        P(expert, row, None),
        P(expert, None, None),
        P(expert + row, None, None),
    )
    out_specs = (P(expert, row, None), P(expert, row, None))
    return jax.shard_map(local, mesh=grid, in_specs=in_specs, out_specs=out_specs, check_vma=False)
```

```python
import functools

import jax
import jax.numpy as jnp
from jax import lax
from jax.experimental import pallas as pl
from jax.experimental.pallas import tpu as pltpu
from jax.sharding import Mesh, PartitionSpec as P

NX, NZ, NY, NC = 4, 8, 4, 2
EXP_DEV = 8
CAP = 12
TOK = 256
LANES = 128
FEAT = 896
WIDE = FEAT + LANES
ROWS = TOK + 16
CHUNKS = (1, 2, 2, 2, 1)
PAIR = 4 * CAP
LAST = EXP_DEV * CAP
FOLD = 6
F32 = jnp.float32
BF16 = jnp.bfloat16


def params(mebibytes):
    return pltpu.CompilerParams(vmem_limit_bytes=mebibytes * 1024 * 1024)


def vmem():
    return pl.BlockSpec(memory_space=pltpu.VMEM)


def smem():
    return pl.BlockSpec(memory_space=pltpu.SMEM)


def cost(micros):
    return pl.CostEstimate(flops=0, bytes_accessed=int(3.69e6 * micros), transcendentals=0)


def routing_rows(routing_t):
    listed = routing_t.astype(F32)
    return jnp.concatenate([listed, jnp.full(listed.shape, -1.0, F32)], axis=0).astype(BF16)


def halves_kernel(tokens_ref, out_ref):
    for copy in range(NY * NC):
        out_ref[copy] = tokens_ref[:, copy % NC * LANES:(copy % NC + 1) * LANES]


def payload_kernel(tokens_ref, routing_ref, out_ref):
    out_ref[0:TOK, :] = tokens_ref[...]
    out_ref[TOK:ROWS, :] = jnp.zeros((16, FEAT), BF16)
    out_ref[TOK:ROWS, 0:TOK] = routing_rows(routing_ref[...])


def join_kernel(forward_ref, backward_ref, edge_ref, *outs):
    for block, out in zip((forward_ref, backward_ref), outs):
        out[:, 0:FEAT] = block[...]
        out[0:TOK, FEAT:WIDE] = edge_ref[...]
        out[TOK:ROWS, FEAT:WIDE] = jnp.zeros((16, LANES), BF16)


def ranks(listed, x_index, z_index):
    line = lax.broadcasted_iota(jnp.int32, (NX * EXP_DEV, TOK), 0)
    label = EXP_DEV * (((x_index + line // EXP_DEV) % NX) * NZ + z_index) + line % EXP_DEV
    label = label.astype(F32)
    member = jnp.zeros((NX * EXP_DEV, TOK), F32)
    for slot in range(8):
        member = member + jnp.where(listed[slot:slot + 1, :] == label, 1.0, 0.0)
    row = lax.broadcasted_iota(jnp.int32, (TOK, TOK), 0)
    column = lax.broadcasted_iota(jnp.int32, (TOK, TOK), 1)
    upto = jnp.where(row <= column, 1.0, 0.0).astype(BF16)
    running = jnp.dot(member.astype(BF16), upto, preferred_element_type=F32)
    return member, member * running


def selectors(rank, count, spot):
    size = count * EXP_DEV * CAP
    shape = (NX * size, NX * EXP_DEV)
    row = lax.broadcasted_iota(jnp.int32, shape, 0)
    column = lax.broadcasted_iota(jnp.int32, shape, 1)
    inside = row % size
    if count == 1:
        expert = inside // CAP
        mine = row >= 0
    else:
        expert = 2 * (inside // (2 * count * CAP)) + (inside % (2 * CAP)) // CAP
        mine = (inside // (2 * CAP)) % count == spot
    match = jnp.logical_and(column == (row // size) * EXP_DEV + expert, mine)
    spread = jnp.where(match, 1.0, 0.0).astype(BF16)
    wide = jnp.dot(spread, rank.astype(BF16), preferred_element_type=F32)
    want = (lax.broadcasted_iota(jnp.int32, (NX * size, TOK), 0) % CAP + 1).astype(F32)
    return jnp.where(wide == want, 1.0, 0.0).astype(BF16)


def fold(rows, out, k, begin):
    for part in range(rows.shape[0] // 16):
        line, lane = begin + part // FOLD * 16, part % FOLD * LANES
        out[line:line + 16, lane:lane + LANES] = rows[part * 16:part * 16 + 16, :]


def choose(select_ref, values, size):
    total = None
    for spot, value in enumerate(values):
        picked = jnp.dot(select_ref[spot], value, preferred_element_type=F32)
        total = picked if total is None else total + picked
    total = total.astype(BF16)
    return [total[k * size:(k + 1) * size, :] for k in range(NX)]


def pack_kernel(chunk, place_ref, before_ref, *refs):
    count = CHUNKS[chunk]
    size = count * LAST
    blocks, refs = refs[:count], refs[count:]
    counts_ref, select_ref, outs = refs[-NX - 2], refs[-NX - 1], refs[-NX:]
    extra = refs[:-NX - 2]
    counts = before_ref[...]
    for spot, block in enumerate(blocks):
        listed = block[TOK:ROWS, 0:TOK].astype(F32)
        member, rank = ranks(listed, place_ref[0], place_ref[1])
        counts = counts + jnp.sum(member, axis=1, keepdims=True)
        select_ref[spot] = selectors(rank, count, spot)
    counts_ref[...] = counts
    features = choose(select_ref, [block[0:TOK, 0:FEAT] for block in blocks], size)
    for k, out in enumerate(outs):
        out[0:size, 0:FEAT] = features[k]
    if chunk == 2:
        older_ref, old_ref, edge_ref = extra
        near = choose(old_ref, [block[0:TOK, FEAT:WIDE] for block in blocks], 2 * LAST)
        own = choose(older_ref, [edge_ref[...]], LAST)
        for k, out in enumerate(outs):
            out[0:size, FEAT:WIDE] = near[k]
            fold(own[k], out, k, size)
    elif chunk == 3:
        old_ref, = extra
        near = choose(old_ref, [block[0:TOK, FEAT:WIDE] for block in blocks], 2 * LAST)
        for k, out in enumerate(outs):
            out[0:size, FEAT:WIDE] = near[k]
    elif chunk == 4:
        old_ref, back_ref, end_ref = extra
        near = choose(old_ref, [blocks[0][0:TOK, FEAT:WIDE], back_ref[...]], 2 * LAST)
        end = choose(select_ref, [end_ref[...]], LAST)
        for k, out in enumerate(outs):
            out[0:size, FEAT:WIDE] = end[k]
            fold(near[k], out, k, size)
            mine = counts[k * EXP_DEV:(k + 1) * EXP_DEV, :]
            out[size:size + 16, FOLD * LANES:FEAT] = jnp.concatenate([mine, mine], axis=0).astype(BF16)


SHAPES = ((LAST, FEAT), (2 * LAST, FEAT), (2 * LAST + 16, WIDE), (2 * LAST, WIDE), (LAST + 32, WIDE))


def pack(chunk, place, before, blocks, *extra):
    count = len(blocks)
    size = count * LAST
    counts, select, *packed = pl.pallas_call(
        functools.partial(pack_kernel, chunk),
        out_shape=[
            jax.ShapeDtypeStruct((NX * EXP_DEV, LANES), F32),
            jax.ShapeDtypeStruct((count, NX * size, TOK), BF16),
        ]
        + [jax.ShapeDtypeStruct(SHAPES[chunk], BF16)] * NX,
        in_specs=[smem()] + [vmem()] * (1 + count + len(extra)),
        out_specs=[vmem()] * (2 + NX),
        compiler_params=params(16),
        cost_estimate=cost(1 + count),
        name="pack_%d" % chunk,
    )(place, before, *blocks, *extra)
    return counts, select, packed


def dot(left, right):
    return jnp.dot(left, right, precision=lax.Precision.HIGHEST, preferred_element_type=F32)


def invert(factor):
    width = factor.shape[0]
    row = lax.broadcasted_iota(jnp.int32, (width, width), 0)
    column = lax.broadcasted_iota(jnp.int32, (width, width), 1)
    diagonal = jnp.where(row == column, factor, 0.0)
    across = 1.0 / jnp.sum(diagonal, axis=0, keepdims=True)
    down = 1.0 / jnp.sum(diagonal, axis=1, keepdims=True)

    def level(span):
        same = row // (2 * span) == column // (2 * span)
        return jnp.where(jnp.logical_and(same, row // span < column // span), factor, 0.0)

    result = jnp.where(row == column, across, 0.0) - down * level(1) * across
    span = 2
    while span < width:
        result = result - dot(dot(result, level(span)), result)
        span *= 2
    return result


def inverse_kernel(factor_ref, out_ref):
    near = invert(factor_ref[0, 0:LANES, 0:LANES])
    far = invert(factor_ref[0, LANES:TOK, LANES:TOK])
    corner = -dot(dot(near, factor_ref[0, 0:LANES, LANES:TOK]), far)
    for copy in range(NY * NC):
        out_ref[copy, 0:LANES, 0:LANES] = near
        out_ref[copy, LANES:TOK, LANES:TOK] = far
        out_ref[copy, LANES:TOK, 0:LANES] = jnp.zeros((LANES, LANES), F32)
        out_ref[copy, 0:LANES, LANES:TOK] = corner


def split(value):
    high = value.astype(BF16)
    return high, (value - high.astype(F32)).astype(BF16)


def errors_kernel(weights_ref, indices_ref, codebook_ref, inverse_ref, out_ref):
    picked = indices_ref[0]
    rows, pairs = picked.shape
    book = codebook_ref[0].astype(F32)
    book = jnp.concatenate([book, jnp.zeros(book.shape, F32)], axis=1)
    coords = [
        jnp.take_along_axis(jnp.broadcast_to(book[c:c + 1, :], (rows, pairs)), picked, axis=1)
        for c in range(2)
    ]
    both = jnp.concatenate(coords, axis=1).astype(BF16)
    row = lax.broadcasted_iota(jnp.int32, (2 * pairs, 2 * pairs), 0)
    column = lax.broadcasted_iota(jnp.int32, (2 * pairs, 2 * pairs), 1)
    weave = jnp.where(column == 2 * (row % pairs) + row // pairs, 1.0, 0.0).astype(BF16)
    decoded = jnp.dot(both, weave, preferred_element_type=F32)
    residual_high, residual_low = split(weights_ref[0].astype(F32) - decoded)
    inverse_high, inverse_low = split(inverse_ref[0])
    total = jnp.dot(residual_low, inverse_high, preferred_element_type=F32)
    total = total + jnp.dot(residual_high, inverse_low, preferred_element_type=F32)
    out_ref[0] = total + jnp.dot(residual_high, inverse_high, preferred_element_type=F32)


def hessian_kernel(place_ref, *refs):
    pieces = NX * len(CHUNKS)
    messages, windows_of, out_ref = refs[:pieces], refs[pieces:-1], refs[-1]
    pair = pl.program_id(0)
    first = place_ref[2] == 0
    row = lax.broadcasted_iota(jnp.int32, (PAIR, TOK), 0)
    single = row // CAP - 2 * (pair % 2)
    double = (row % (2 * CAP)) // CAP
    features, windows = [], []
    for k in range(NX):
        for c, count in enumerate(CHUNKS):
            step = pair // (3 - count)
            where = pl.ds(pl.multiple_of(step * PAIR, 16), PAIR)
            features.append(messages[k * len(CHUNKS) + c][where, 0:FEAT])
            mine_ref, other_ref = windows_of[0:2] if c < 3 else windows_of[2:4]
            begin = WINDOW_ROWS[c] + k * count * LAST
            where = pl.ds(pl.multiple_of(begin + step * PAIR, 16), PAIR)
            near, far = mine_ref[where, :].astype(F32), other_ref[where, :].astype(F32)
            both = jnp.concatenate(
                [jnp.where(first, near, far), jnp.where(first, far, near)], axis=1
            )
            owner = single if count == 1 else double
            windows.append(
                jnp.concatenate(
                    [jnp.where(owner == e, both, 0.0) for e in range(2)], axis=1
                ).astype(BF16)
            )
    product = lax.dot_general(
        jnp.concatenate(features, axis=0),
        jnp.concatenate(windows, axis=0),
        (((0,), (0,)), ((), ())),
        preferred_element_type=F32,
    )
    counts = jnp.zeros((16, LANES), F32)
    for k in range(NX):
        ref = messages[k * len(CHUNKS) + 4]
        counts = counts + ref[LAST:LAST + 16, FOLD * LANES:FEAT].astype(F32)
    line = lax.broadcasted_iota(jnp.int32, counts.shape, 0)
    for e in range(2):
        count = jnp.sum(jnp.where(line == 2 * pair + e, counts, 0.0), axis=0, keepdims=True)
        scale = 2.0 / count
        scale = jnp.concatenate([scale, scale], axis=1)
        out_ref[e] = product[:, e * TOK:(e + 1) * TOK] * scale


WINDOW_ROWS = (0, 4 * LAST, 12 * LAST, 0, 8 * LAST)


def unfold(ref, out_ref, source, begin, rows):
    for part in range(rows // 16):
        line, lane = source + part // FOLD * 16, part % FOLD * LANES
        out_ref[begin + part * 16:begin + part * 16 + 16, :] = ref[line:line + 16, lane:lane + LANES]


def early_kernel(*refs):
    second, third, out_ref = refs[0:NX], refs[NX:2 * NX], refs[-1]
    for k in range(NX):
        unfold(second[k], out_ref, 2 * LAST, WINDOW_ROWS[0] + k * LAST, LAST)
        begin = WINDOW_ROWS[1] + k * 2 * LAST
        out_ref[begin:begin + 2 * LAST, :] = second[k][0:2 * LAST, FEAT:WIDE]
        begin = WINDOW_ROWS[2] + k * 2 * LAST
        out_ref[begin:begin + 2 * LAST, :] = third[k][:, FEAT:WIDE]


def late_kernel(*refs):
    last, out_ref = refs[0:NX], refs[-1]
    for k in range(NX):
        unfold(last[k], out_ref, LAST, WINDOW_ROWS[3] + k * 2 * LAST, 2 * LAST)
        begin = WINDOW_ROWS[4] + k * LAST
        out_ref[begin:begin + LAST, :] = last[k][0:LAST, FEAT:WIDE]


def shifted(size, step):
    return [(i, (i + step) % size) for i in range(size)]


def move(value, axis, size, step):
    return lax.ppermute(value, axis, shifted(size, step))


def tie(*values):
    return lax.optimization_barrier(values)


def send(packed):
    return [packed[0]] + [move(packed[k], "x", NX, k) for k in (1, 2, 3)]


def swap(kernel, rows, values):
    mine = pl.pallas_call(
        kernel,
        out_shape=jax.ShapeDtypeStruct((rows, LANES), BF16),
        in_specs=[vmem()] * len(values),
        out_specs=vmem(),
        compiler_params=params(8),
        cost_estimate=cost(0.5),
        name="window_half",
    )(*values)
    return mine, move(mine, "core", NC, 1)


def local(tokens, routing, weights, indices, codebook, hinv_panel):
    x_index, z_index = lax.axis_index("x"), lax.axis_index("z")
    core = lax.axis_index("core")
    place = jnp.stack([x_index, z_index, core]).astype(jnp.int32)
    payload = pl.pallas_call(
        payload_kernel,
        out_shape=jax.ShapeDtypeStruct((ROWS, FEAT), BF16),
        in_specs=[vmem()] * 2,
        out_specs=vmem(),
        compiler_params=params(4),
        cost_estimate=cost(0.3),
        name="payload",
    )(tokens, routing.T)
    f1, b1 = move(payload, "z", NZ, 1), move(payload, "z", NZ, -1)
    halves = pl.pallas_call(
        halves_kernel,
        grid=(1,),
        out_shape=jax.ShapeDtypeStruct((NY * NC, TOK, LANES), BF16),
        in_specs=[pl.BlockSpec((TOK, 2 * LANES), lambda i: (0, 0))],
        out_specs=pl.BlockSpec((NY * NC, TOK, LANES), lambda i: (0, 0, 0)),
        compiler_params=params(4),
        cost_estimate=cost(0.3),
        name="halves",
    )(tokens)
    edge = lax.all_to_all(halves, ("y", "core"), 0, 0, tiled=True)[0]
    counts, select0, packed = pack(
        0, place, jnp.zeros((NX * EXP_DEV, LANES), F32), [payload]
    )

    f1, b1, counts, edge, *packed = tie(f1, b1, counts, edge, *packed)
    joined_f, joined_b = pl.pallas_call(
        join_kernel,
        out_shape=[jax.ShapeDtypeStruct((ROWS, WIDE), BF16)] * 2,
        in_specs=[vmem()] * 3,
        out_specs=[vmem()] * 2,
        compiler_params=params(8),
        cost_estimate=cost(0.6),
        name="join",
    )(f1, b1, edge)
    f2, b2 = move(joined_f, "z", NZ, 1), move(joined_b, "z", NZ, -1)
    sent = [send(packed)]
    counts, select1, packed = pack(1, place, counts, [f1, b1])
    sent.append(send(packed))

    f2, b2, counts, *sent[0] = tie(f2, b2, counts, *sent[0])
    f3, b3 = move(f2, "z", NZ, 1), move(b2, "z", NZ, -1)
    counts, select2, packed = pack(2, place, counts, [f2, b2], select0, select1, edge)
    sent.append(send(packed))
    hinv_panel, counts = tie(hinv_panel, counts)
    inverse = pl.pallas_call(
        inverse_kernel,
        out_shape=jax.ShapeDtypeStruct((NY * NC, TOK, TOK), F32),
        in_specs=[vmem()],
        out_specs=vmem(),
        compiler_params=params(8),
        cost_estimate=cost(7.5),
        name="inverse",
    )(hinv_panel)

    f3, b3, counts, inverse, *sent[1] = tie(f3, b3, counts, inverse, *sent[1])
    inverses = lax.all_to_all(inverse, ("y", "core"), 0, 0, tiled=True)
    f4 = move(f3, "z", NZ, 1)
    back = move(b3[0:TOK, FEAT:WIDE], "z", NZ, -1)
    counts, select3, packed = pack(3, place, counts, [f3, b3], select2)
    sent.append(send(packed))

    f4, back, counts, *sent[2] = tie(f4, back, counts, *sent[2])
    end = move(f4[0:TOK, FEAT:WIDE], "z", NZ, 1)
    counts, _, packed = pack(4, place, counts, [f4], select3, back, end)
    weights, packed[0] = tie(weights, packed[0])
    sent.append(send(packed))
    early = swap(early_kernel, 20 * LAST, [*sent[2], *sent[3]])
    experts, rows, width = weights.shape
    pairs = indices.shape[2]
    errors = pl.pallas_call(
        errors_kernel,
        grid=(experts,),
        out_shape=jax.ShapeDtypeStruct(weights.shape, F32),
        in_specs=[
            pl.BlockSpec((1, rows, width), lambda e: (e, 0, 0)),
            pl.BlockSpec((1, rows, pairs), lambda e: (e, 0, 0)),
            pl.BlockSpec((1,) + codebook.shape[1:], lambda e: (e, 0, 0)),
            pl.BlockSpec((1, width, width), lambda e: (e, 0, 0)),
        ],
        out_specs=pl.BlockSpec((1, rows, width), lambda e: (e, 0, 0)),
        compiler_params=params(8),
        cost_estimate=cost(5),
        name="errors",
    )(weights, indices, codebook, inverses)

    errors, *rest = tie(errors, *sent[4], *sent[3])
    sent[4], sent[3] = rest[:NX], rest[NX:]
    late = swap(late_kernel, 12 * LAST, sent[4])
    operands = [sent[c][k] for k in range(NX) for c in range(len(CHUNKS))]
    operands += [*early, *late]
    hessian = pl.pallas_call(
        hessian_kernel,
        grid=(EXP_DEV // 2,),
        out_shape=jax.ShapeDtypeStruct((EXP_DEV, FEAT, TOK), F32),
        in_specs=[smem()] + [vmem()] * len(operands),
        out_specs=pl.BlockSpec((2, FEAT, TOK), lambda p: (p, 0, 0)),
        compiler_params=params(20),
        cost_estimate=cost(7.5),
        name="hessian",
    )(place, *operands)
    return hessian, errors


def solution(mesh):
    grid = Mesh(mesh.devices.reshape(NX, NZ, NY, NC), ("x", "z", "y", "core"))
    expert, row = ("x", "z"), ("y", "core")
    in_specs = (
        P(expert, row),
        P(expert, None),
        P(expert, row, None),
        P(expert, row, None),
        P(expert, None, None),
        P(expert + row, None, None),
    )
    out_specs = (P(expert, row, None), P(expert, row, None))
    return jax.shard_map(local, mesh=grid, in_specs=in_specs, out_specs=out_specs, check_vma=False)
```

```python
import functools

import jax
import jax.numpy as jnp
from jax import lax
from jax.experimental import pallas as pl
from jax.experimental.pallas import tpu as pltpu
from jax.sharding import Mesh, PartitionSpec as P

NX, NZ, NY, NC = 4, 8, 4, 2
EXP_DEV = 8
CAP = 12
TOK = 256
LANES = 128
FEAT = 896
WIDE = FEAT + LANES
ROWS = TOK + 16
CHUNKS = (1, 2, 2, 2, 1)
PAIR = 4 * CAP
LAST = EXP_DEV * CAP
F32 = jnp.float32
BF16 = jnp.bfloat16


def params(mebibytes):
    return pltpu.CompilerParams(vmem_limit_bytes=mebibytes * 1024 * 1024)


def vmem():
    return pl.BlockSpec(memory_space=pltpu.VMEM)


def smem():
    return pl.BlockSpec(memory_space=pltpu.SMEM)


def cost(micros):
    return pl.CostEstimate(flops=0, bytes_accessed=int(3.69e6 * micros), transcendentals=0)


def routing_rows(routing_t):
    listed = routing_t.astype(F32)
    return jnp.concatenate([listed, jnp.full(listed.shape, -1.0, F32)], axis=0).astype(BF16)


def halves_kernel(tokens_ref, out_ref):
    for copy in range(NY * NC):
        out_ref[copy] = tokens_ref[:, copy % NC * LANES:(copy % NC + 1) * LANES]


def payload_kernel(tokens_ref, routing_ref, out_ref):
    out_ref[0:TOK, :] = tokens_ref[...]
    out_ref[TOK:ROWS, :] = jnp.zeros((16, FEAT), BF16)
    out_ref[TOK:ROWS, 0:TOK] = routing_rows(routing_ref[...])


def join_kernel(*refs):
    count = len(refs) // 3
    for block, edge, out in zip(refs[:count], refs[count:2 * count], refs[2 * count:]):
        out[:, 0:FEAT] = block[...]
        out[0:TOK, FEAT:WIDE] = edge[...]
        out[TOK:ROWS, FEAT:WIDE] = jnp.zeros((16, LANES), BF16)


def join(blocks, edges):
    count = len(blocks)
    return list(pl.pallas_call(
        join_kernel,
        out_shape=[jax.ShapeDtypeStruct((ROWS, WIDE), BF16)] * count,
        in_specs=[vmem()] * (2 * count),
        out_specs=[vmem()] * count,
        compiler_params=params(8),
        cost_estimate=cost(0.3 * count),
        name="join_%d" % count,
    )(*blocks, *edges))


def gather_kernel(*refs):
    begin = 0
    for ref in refs[:-1]:
        rows = ref.shape[0] // PAIR * PAIR
        refs[-1][begin:begin + rows, :] = ref[0:rows, FEAT:WIDE]
        begin += rows


def ranks(listed, x_index, z_index):
    line = lax.broadcasted_iota(jnp.int32, (NX * EXP_DEV, TOK), 0)
    label = EXP_DEV * (((x_index + line // EXP_DEV) % NX) * NZ + z_index) + line % EXP_DEV
    label = label.astype(F32)
    member = jnp.zeros((NX * EXP_DEV, TOK), F32)
    for slot in range(8):
        member = member + jnp.where(listed[slot:slot + 1, :] == label, 1.0, 0.0)
    row = lax.broadcasted_iota(jnp.int32, (TOK, TOK), 0)
    column = lax.broadcasted_iota(jnp.int32, (TOK, TOK), 1)
    upto = jnp.where(row <= column, 1.0, 0.0).astype(BF16)
    running = jnp.dot(member.astype(BF16), upto, preferred_element_type=F32)
    return member, member * running


def selectors(rank, count, spot):
    size = count * EXP_DEV * CAP
    shape = (NX * size, NX * EXP_DEV)
    row = lax.broadcasted_iota(jnp.int32, shape, 0)
    column = lax.broadcasted_iota(jnp.int32, shape, 1)
    inside = row % size
    if count == 1:
        expert = inside // CAP
        mine = row >= 0
    else:
        expert = 2 * (inside // (2 * count * CAP)) + (inside % (2 * CAP)) // CAP
        mine = (inside // (2 * CAP)) % count == spot
    match = jnp.logical_and(column == (row // size) * EXP_DEV + expert, mine)
    spread = jnp.where(match, 1.0, 0.0).astype(BF16)
    wide = jnp.dot(spread, rank.astype(BF16), preferred_element_type=F32)
    want = (lax.broadcasted_iota(jnp.int32, (NX * size, TOK), 0) % CAP + 1).astype(F32)
    return jnp.where(wide == want, 1.0, 0.0).astype(BF16)


def pack_kernel(count, last, place_ref, before_ref, *refs):
    blocks, counts_ref, outs = refs[:count], refs[count], refs[count + 1:]
    size = count * EXP_DEV * CAP
    counts = before_ref[...]
    total = None
    for spot, block in enumerate(blocks):
        listed = block[TOK:ROWS, 0:TOK].astype(F32)
        member, rank = ranks(listed, place_ref[0], place_ref[1])
        counts = counts + jnp.sum(member, axis=1, keepdims=True)
        picked = jnp.dot(
            selectors(rank, count, spot), block[0:TOK, :], preferred_element_type=F32
        )
        total = picked if total is None else total + picked
    counts_ref[...] = counts
    for k, out in enumerate(outs):
        out[0:size, :] = total[k * size:(k + 1) * size, :].astype(BF16)
        if last:
            mine = counts[k * EXP_DEV:(k + 1) * EXP_DEV, 0:1]
            mine = jnp.broadcast_to(jnp.concatenate([mine, mine], axis=0), (16, WIDE))
            out[size:size + 16, :] = mine.astype(BF16)


def pack(place, before, blocks, last):
    count = len(blocks)
    size = count * EXP_DEV * CAP + (16 if last else 0)
    counts, *packed = pl.pallas_call(
        functools.partial(pack_kernel, count, last),
        out_shape=[jax.ShapeDtypeStruct((NX * EXP_DEV, LANES), F32)]
        + [jax.ShapeDtypeStruct((size, WIDE), BF16)] * NX,
        in_specs=[smem()] + [vmem()] * (1 + count),
        out_specs=[vmem()] * (1 + NX),
        compiler_params=params(8),
        cost_estimate=cost(1 + count),
        name="pack_%d" % count,
    )(place, before, *blocks)
    return counts, packed


def dot(left, right):
    return jnp.dot(left, right, precision=lax.Precision.HIGHEST, preferred_element_type=F32)


def invert(factor):
    width = factor.shape[0]
    row = lax.broadcasted_iota(jnp.int32, (width, width), 0)
    column = lax.broadcasted_iota(jnp.int32, (width, width), 1)
    diagonal = jnp.where(row == column, factor, 0.0)
    across = 1.0 / jnp.sum(diagonal, axis=0, keepdims=True)
    down = 1.0 / jnp.sum(diagonal, axis=1, keepdims=True)

    def level(span):
        same = row // (2 * span) == column // (2 * span)
        return jnp.where(jnp.logical_and(same, row // span < column // span), factor, 0.0)

    result = jnp.where(row == column, across, 0.0) - down * level(1) * across
    span = 2
    while span < width:
        result = result - dot(dot(result, level(span)), result)
        span *= 2
    return result


def inverse_kernel(factor_ref, out_ref):
    near = invert(factor_ref[0, 0:LANES, 0:LANES])
    far = invert(factor_ref[0, LANES:TOK, LANES:TOK])
    corner = -dot(dot(near, factor_ref[0, 0:LANES, LANES:TOK]), far)
    for copy in range(NY * NC):
        out_ref[copy, 0:LANES, 0:LANES] = near
        out_ref[copy, LANES:TOK, LANES:TOK] = far
        out_ref[copy, LANES:TOK, 0:LANES] = jnp.zeros((LANES, LANES), F32)
        out_ref[copy, 0:LANES, LANES:TOK] = corner


def split(value):
    high = value.astype(BF16)
    return high, (value - high.astype(F32)).astype(BF16)


def errors_kernel(weights_ref, indices_ref, codebook_ref, inverse_ref, out_ref):
    picked = indices_ref[0]
    rows, pairs = picked.shape
    book = codebook_ref[0].astype(F32)
    book = jnp.concatenate([book, jnp.zeros(book.shape, F32)], axis=1)
    coords = [
        jnp.take_along_axis(jnp.broadcast_to(book[c:c + 1, :], (rows, pairs)), picked, axis=1)
        for c in range(2)
    ]
    both = jnp.concatenate(coords, axis=1).astype(BF16)
    row = lax.broadcasted_iota(jnp.int32, (2 * pairs, 2 * pairs), 0)
    column = lax.broadcasted_iota(jnp.int32, (2 * pairs, 2 * pairs), 1)
    weave = jnp.where(column == 2 * (row % pairs) + row // pairs, 1.0, 0.0).astype(BF16)
    decoded = jnp.dot(both, weave, preferred_element_type=F32)
    residual_high, residual_low = split(weights_ref[0].astype(F32) - decoded)
    inverse_high, inverse_low = split(inverse_ref[0])
    total = jnp.dot(residual_low, inverse_high, preferred_element_type=F32)
    total = total + jnp.dot(residual_high, inverse_low, preferred_element_type=F32)
    out_ref[0] = total + jnp.dot(residual_high, inverse_high, preferred_element_type=F32)


def hessian_kernel(chunks, place_ref, *refs):
    last = 4 in chunks
    pieces = NX * len(chunks)
    messages, others, out_ref = refs[:pieces], refs[pieces:2 * pieces], refs[-1]
    counted = refs[2 * pieces:2 * pieces + NX]
    pair = pl.program_id(0)
    first = place_ref[2] == 0
    row = lax.broadcasted_iota(jnp.int32, (PAIR, TOK), 0)
    single = row // CAP - 2 * (pair % 2)
    double = (row % (2 * CAP)) // CAP
    features, windows = [], []
    for k in range(NX):
        for c, chunk in enumerate(chunks):
            count = CHUNKS[chunk]
            ref = messages[k * len(chunks) + c]
            features.append(ref[:, 0:FEAT])
            near = ref[:, FEAT:WIDE].astype(F32)
            far = others[k * len(chunks) + c][...].astype(F32)
            both = jnp.concatenate(
                [jnp.where(first, near, far), jnp.where(first, far, near)], axis=1
            )
            owner = single if count == 1 else double
            windows.append(
                jnp.concatenate(
                    [jnp.where(owner == e, both, 0.0) for e in range(2)], axis=1
                ).astype(BF16)
            )
    product = lax.dot_general(
        jnp.concatenate(features, axis=0),
        jnp.concatenate(windows, axis=0),
        (((0,), (0,)), ((), ())),
        preferred_element_type=F32,
    )
    if not last:
        for e in range(2):
            out_ref[e] = product[:, e * TOK:(e + 1) * TOK]
        return
    counts = counted[0][...].astype(F32)
    for ref in counted[1:]:
        counts = counts + ref[...].astype(F32)
    line = lax.broadcasted_iota(jnp.int32, counts.shape, 0)
    for e in range(2):
        count = jnp.sum(jnp.where(line == 2 * pair + e, counts, 0.0), axis=0, keepdims=True)
        out_ref[e] = (product[:, e * TOK:(e + 1) * TOK] + refs[-2][e]) * (2.0 / count)


def shifted(size, step):
    return [(i, (i + step) % size) for i in range(size)]


def hessian_part(place, sent, group, chunks, before):
    operands, specs, other_specs = [], [], []
    begins, begin = {}, 0
    for c in chunks:
        for k in range(NX):
            begins[k, c] = begin
            begin += CHUNKS[c] * LAST
    for k in range(NX):
        for c in chunks:
            share = 2 // CHUNKS[c]
            operands.append(sent[c][k])
            specs.append(pl.BlockSpec((PAIR, WIDE), lambda p, s=share: (p // s, 0)))
            other_specs.append(
                pl.BlockSpec((PAIR, LANES), lambda p, s=share, b=begins[k, c] // PAIR: (b + p // s, 0))
            )
    pieces = len(operands)
    operands += [group] * pieces
    specs += other_specs
    block = pl.BlockSpec((2, FEAT, TOK), lambda p: (p, 0, 0))
    if before is not None:
        operands += [*sent[4], before]
        specs += [pl.BlockSpec((16, TOK), lambda p: (LAST // 16, 0))] * NX + [block]
    return pl.pallas_call(
        functools.partial(hessian_kernel, chunks),
        grid=(EXP_DEV // 2,),
        out_shape=jax.ShapeDtypeStruct((EXP_DEV, FEAT, TOK), F32),
        in_specs=[smem()] + specs,
        out_specs=block,
        compiler_params=params(24),
        cost_estimate=cost(5),
        name="hessian_%d" % len(chunks),
    )(place, *operands)


def move(value, axis, size, step):
    return lax.ppermute(value, axis, shifted(size, step))


def tie(*values):
    return lax.optimization_barrier(values)


def send(packed):
    return [packed[0]] + [move(packed[k], "x", NX, k) for k in (1, 2, 3)]


def swap(chunks):
    values = [value for chunk in chunks for value in chunk]
    rows = sum(value.shape[0] // PAIR * PAIR for value in values)
    held = pl.pallas_call(
        gather_kernel,
        out_shape=jax.ShapeDtypeStruct((rows, LANES), BF16),
        in_specs=[vmem()] * len(values),
        out_specs=vmem(),
        compiler_params=params(8),
        cost_estimate=cost(0.5),
        name="window_half",
    )(*values)
    return move(held, "core", NC, 1)


def local(tokens, routing, weights, indices, codebook, hinv_panel):
    x_index, z_index = lax.axis_index("x"), lax.axis_index("z")
    core = lax.axis_index("core")
    place = jnp.stack([x_index, z_index, core]).astype(jnp.int32)
    payload = pl.pallas_call(
        payload_kernel,
        out_shape=jax.ShapeDtypeStruct((ROWS, FEAT), BF16),
        in_specs=[vmem()] * 2,
        out_specs=vmem(),
        compiler_params=params(4),
        cost_estimate=cost(0.3),
        name="payload",
    )(tokens, routing.T)
    f1, b1 = move(payload, "z", NZ, 1), move(payload, "z", NZ, -1)
    halves = pl.pallas_call(
        halves_kernel,
        grid=(1,),
        out_shape=jax.ShapeDtypeStruct((NY * NC, TOK, LANES), BF16),
        in_specs=[pl.BlockSpec((TOK, 2 * LANES), lambda i: (0, 0))],
        out_specs=pl.BlockSpec((NY * NC, TOK, LANES), lambda i: (0, 0, 0)),
        compiler_params=params(4),
        cost_estimate=cost(0.3),
        name="halves",
    )(tokens)
    edge = lax.all_to_all(halves, ("y", "core"), 0, 0, tiled=True)[0]
    edge_f, edge_b = move(edge, "z", NZ, 1), move(edge, "z", NZ, -1)
    counts, packed = pack(
        place, jnp.zeros((NX * EXP_DEV, LANES), F32), join([payload], [edge]), False
    )

    f1, b1, edge_f, edge_b, counts, *packed = tie(f1, b1, edge_f, edge_b, counts, *packed)
    f1, b1 = join([f1, b1], [edge_f, edge_b])
    f2, b2 = move(f1, "z", NZ, 1), move(b1, "z", NZ, -1)
    sent = [send(packed)]
    counts, packed = pack(place, counts, [f1, b1], False)
    sent.append(send(packed))

    f2, b2, counts, *sent[0] = tie(f2, b2, counts, *sent[0])
    f3, b3 = move(f2, "z", NZ, 1), move(b2, "z", NZ, -1)
    counts, packed = pack(place, counts, [f2, b2], False)
    sent.append(send(packed))
    hinv_panel, counts = tie(hinv_panel, counts)
    inverse = pl.pallas_call(
        inverse_kernel,
        out_shape=jax.ShapeDtypeStruct((NY * NC, TOK, TOK), F32),
        in_specs=[vmem()],
        out_specs=vmem(),
        compiler_params=params(8),
        cost_estimate=cost(7.5),
        name="inverse",
    )(hinv_panel)

    f3, b3, counts, inverse, *sent[1] = tie(f3, b3, counts, inverse, *sent[1])
    inverses = lax.all_to_all(inverse, ("y", "core"), 0, 0, tiled=True)
    f4 = move(f3, "z", NZ, 1)
    early = swap(sent[0:2])
    counts, packed = pack(place, counts, [f3, b3], False)
    sent.append(send(packed))

    f4, counts, early, *sent[2] = tie(f4, counts, early, *sent[2])
    counts, packed = pack(place, counts, [f4], True)
    weights, packed[0] = tie(weights, packed[0])
    sent.append(send(packed))
    experts, rows, width = weights.shape
    pairs = indices.shape[2]
    errors = pl.pallas_call(
        errors_kernel,
        grid=(experts,),
        out_shape=jax.ShapeDtypeStruct(weights.shape, F32),
        in_specs=[
            pl.BlockSpec((1, rows, width), lambda e: (e, 0, 0)),
            pl.BlockSpec((1, rows, pairs), lambda e: (e, 0, 0)),
            pl.BlockSpec((1,) + codebook.shape[1:], lambda e: (e, 0, 0)),
            pl.BlockSpec((1, width, width), lambda e: (e, 0, 0)),
        ],
        out_specs=pl.BlockSpec((1, rows, width), lambda e: (e, 0, 0)),
        compiler_params=params(8),
        cost_estimate=cost(5),
        name="errors",
    )(weights, indices, codebook, inverses)

    errors, place = tie(errors, place)
    hessian = hessian_part(place, sent, early, (0, 1), None)
    hessian, *rest = tie(hessian, *sent[3], *sent[4])
    sent[3], sent[4] = rest[:NX], rest[NX:]
    late = swap(sent[2:5])
    hessian = hessian_part(place, sent, late, (2, 3, 4), hessian)
    return hessian, errors


def solution(mesh):
    grid = Mesh(mesh.devices.reshape(NX, NZ, NY, NC), ("x", "z", "y", "core"))
    expert, row = ("x", "z"), ("y", "core")
    in_specs = (
        P(expert, row),
        P(expert, None),
        P(expert, row, None),
        P(expert, row, None),
        P(expert, None, None),
        P(expert + row, None, None),
    )
    out_specs = (P(expert, row, None), P(expert, row, None))
    return jax.shard_map(local, mesh=grid, in_specs=in_specs, out_specs=out_specs, check_vma=False)
```
